32 devices in a mesh: node: 2 (over y), space: 16 (over z, x, core).
Axes of the slice: x: 2, y: 2, z: 4, core: 2. Of those that a mesh axis runs over, the one named last changes fastest.
Arguments:
- grain_ids: int32 [64, 16, 128], P('space'), may hold values from 0 to 7
- peak_heat: float32 [64, 16, 128], P('space'), may hold values from 0.5 to 1
Outputs:
- node_states: float32 [2, 8, 64, 16, 128], P('node', None, 'space')
The draws below stay inside these ranges and needn't reach their ends.
All inputs are finite; a program needn't handle non-finite values.
Results may differ from the reference program's by a relative error of at most 0.0001.
Values sent between devices are 32-bit elements; how exact they have to be, the bound alone decides.
A program may use at most 64 MiB of HBM per device.

```python
import math
import jax
import jax.numpy as jnp
import numpy as np
from jax import lax

P_SIZE = 8
NODES = 2
CX = 128
CY = 16
NZ = 64
SWEEPS = 3
JACOBI = 2
STEPS = 2


def with_ends(values, key, smallest, top_value):
    dims = values.shape
    spot = [jax.random.randint(jax.random.fold_in(key, axis), (), 0, dims[axis]) for axis in range(len(dims))]
    values = values.at[tuple(spot)].set(smallest)
    longest = dims.index(max(dims))
    spot[longest] = (spot[longest] + 1) % dims[longest]
    return values.at[tuple(spot)].set(top_value)


def block_scale(rng, shape, pieces, low, top_value):
    loudness = 1.0
    for position, blocks in pieces:
        draws = jax.random.uniform(jax.random.fold_in(jax.random.fold_in(rng, 6), position), (blocks,), jnp.float32, low / len(pieces), top_value / len(pieces))
        loudness = loudness * jnp.repeat(jnp.exp(draws), shape[position] // blocks).reshape((-1,) + (1,) * (len(shape) - 1 - position))
    return loudness


def setup_inputs(seed: int = 0) -> dict:
    splits = jax.random.split(jax.random.key(seed), 3)
    return {
        "grain_ids": with_ends(jax.random.randint(splits[0], (NZ, CY, CX), 0, P_SIZE), jax.random.fold_in(splits[0], 1), 0, P_SIZE - 1).astype(jnp.int32),
        "peak_heat": jnp.clip(0.5 + 0.5 * jax.random.uniform(splits[1], (NZ, CY, CX), jnp.float32) ** block_scale(splits[1], (NZ, CY, CX), ((0, 16),), -0.2, 0.2), 0.5, 1.0),
    }


time_step = 0.25
cross_coef = 1.5
base_heat = 0.45
activation = 3.0


def legendre_pair(count, point):
    before = 1.0
    current = point
    for degree in range(2, count + 1):
        following = ((2 * degree - 1) * point * current - (degree - 1) * before) / degree
        before = current
        current = following
    return current, before


def radau_value(count, point):
    high, low = legendre_pair(count, point)
    high_prev, low_prev = legendre_pair(count - 1, point) if count > 1 else (1.0, 1.0)
    value = high - low
    slope_high = count * (point * high - low) / (point * point - 1.0)
    if count > 1:
        slope_low = (count - 1) * (point * high_prev - low_prev) / (point * point - 1.0)
    else:
        slope_low = 0.0
    return value, slope_high - slope_low


def radau_table(count):
    roots = [1.0]
    for index in range(1, count):
        point = math.cos(2.0 * math.pi * index / (2 * count - 1))
        for repeat in range(100):
            value, slope = radau_value(count, point)
            point = point - value / slope
        roots.append(point)
    roots = sorted(roots)
    times_list = [(value + 1.0) / 2.0 for value in roots]
    times_list[-1] = 1.0
    table = []
    for row_index in range(count):
        upper = times_list[row_index]
        row_values = []
        for column in range(count):
            poly = [1.0]
            for other in range(count):
                if other != column:
                    scale = times_list[column] - times_list[other]
                    shifted = [0.0] + poly
                    scaled = [c * times_list[other] for c in poly] + [0.0]
                    poly = [(shifted[i] - scaled[i]) / scale for i in range(len(shifted))]
            integral_value = 0.0
            for power in range(len(poly)):
                integral_value += poly[power] * upper ** (power + 1) / (power + 1)
            row_values.append(integral_value)
        table.append(row_values)
    return np.array(times_list), np.array(table)


def drive(field):
    squares = field * field
    total = jnp.sum(squares, axis=-4, keepdims=True)
    return -field + squares * field + 2.0 * cross_coef * field * (total - squares)


def neighbours(field):
    result = jnp.roll(field, -1, -3) + jnp.roll(field, 1, -3)
    result = result + jnp.roll(field, -1, -2) + jnp.roll(field, 1, -2)
    return result + jnp.roll(field, -1, -1) + jnp.roll(field, 1, -1)


def heat_mobility(peak, moment):
    middle = 0.5 * time_step * STEPS
    theta = base_heat + (peak - base_heat) * jnp.exp(-((moment - middle) / middle) ** 2)
    return jnp.exp(activation * (1.0 - 1.0 / theta))


def rate(field, mobility):
    return -mobility * (drive(field) - (neighbours(field) - 6.0 * field))


def relax(field, goal, factor):
    return (goal + factor * (neighbours(field) - drive(field))) / (1.0 + 6.0 * factor)


def reference(grain_ids, peak_heat):
    node_times, table = radau_table(NODES)
    times = jnp.asarray(node_times, jnp.float32)
    weights = jnp.asarray(table, jnp.float32)
    orders = jnp.arange(P_SIZE, dtype=jnp.int32)
    start = (grain_ids[None] == orders[:, None, None, None]).astype(jnp.float32)
    taus = times.reshape((NODES, 1, 1, 1, 1))
    states = None
    for step_index in range(STEPS):
        moments = (step_index + times) * time_step
        mobility = heat_mobility(peak_heat[None], moments[:, None, None, None])[:, None]
        factor = time_step * taus * mobility
        rates = rate(start[None], mobility)
        states = jnp.broadcast_to(start[None], rates.shape)
        for sweep_index in range(SWEEPS):
            quad = jnp.tensordot(weights, rates, axes=1, precision=lax.Precision.HIGHEST)
            goal = start[None] + time_step * quad - time_step * taus * rates
            for relax_index in range(JACOBI):
                states = relax(states, goal, factor)
            if sweep_index + 1 < SWEEPS:
                rates = rate(states, mobility)
        start = states[-1]
    return states
```

```python
import functools
import math

import jax
import jax.numpy as jnp
import numpy as np
from jax import lax
from jax.experimental import pallas as pl
from jax.experimental.pallas import tpu as pltpu
from jax.sharding import PartitionSpec as P

P_SIZE = 8
NODE_DEV = 1
SWEEPS = 3
JACOBI = 2
STEPS = 2
STEP_REACH = SWEEPS * JACOBI
REACH = STEPS * STEP_REACH

time_step = 0.25
cross_coef = 1.5
base_heat = 0.45
activation = 3.0

MESH = pl.DeviceIdType.MESH


def legendre_pair(count, point):
    before = 1.0
    current = point
    for degree in range(2, count + 1):
        following = ((2 * degree - 1) * point * current - (degree - 1) * before) / degree
        before = current
        current = following
    return (current, before)


def radau_value(count, point):
    high, low = legendre_pair(count, point)
    high_prev, low_prev = legendre_pair(count - 1, point)
    value = high - low
    slope_high = count * (point * high - low) / (point * point - 1.0)
    slope_low = (count - 1) * (point * high_prev - low_prev) / (point * point - 1.0)
    return (value, slope_high - slope_low)


def radau_table(count):
    roots = [1.0]
    for index in range(1, count):
        point = math.cos(2.0 * math.pi * index / (2 * count - 1))
        for repeat in range(100):
            value, slope = radau_value(count, point)
            point = point - value / slope
        roots.append(point)
    roots = sorted(roots)
    times_list = [(value + 1.0) / 2.0 for value in roots]
    times_list[-1] = 1.0
    table = []
    for row_index in range(count):
        upper = times_list[row_index]
        row_values = []
        for column in range(count):
            poly = [1.0]
            for other in range(count):
                if other != column:
                    scale = times_list[column] - times_list[other]
                    shifted = [0.0] + poly
                    scaled = [c * times_list[other] for c in poly] + [0.0]
                    poly = [(shifted[i] - scaled[i]) / scale for i in range(len(shifted))]
            integral_value = 0.0
            for power in range(len(poly)):
                integral_value += poly[power] * upper ** (power + 1) / (power + 1)
            row_values.append(integral_value)
        table.append(row_values)
    return (np.array(times_list), np.array(table))


def exchange_kernel(count, planes, hops, ids_ref, heat_ref, ext_ref, send, recv):
    me = lax.axis_index("space")
    offsets = [d for k in range(1, hops + 1) for d in (k, -k)]

    def target(offset):
        return {"space": lax.rem(me + offset + count, count)}

    barrier = pltpu.get_barrier_semaphore()
    for offset in offsets:
        pl.semaphore_signal(barrier, inc=1, device_id=target(offset), device_id_type=MESH)
    own = hops * planes
    for z in range(planes):
        for h in range(2):
            rows = pl.ds(h, 8, stride=2)
            ext_ref[own + z, 0, h] = ids_ref[z, rows, :].astype(jnp.float32)
            ext_ref[own + z, 1, h] = heat_ref[z, rows, :]
    pl.semaphore_wait(barrier, len(offsets))
    copies = []
    for index, offset in enumerate(offsets):
        copy = pltpu.make_async_remote_copy(
            src_ref=ext_ref.at[pl.ds(own, planes)],
            dst_ref=ext_ref.at[pl.ds(own - offset * planes, planes)],
            send_sem=send.at[index],
            recv_sem=recv.at[index],
            device_id=target(offset),
            device_id_type=MESH,
        )
        copy.start()
        copies.append(copy)
    for copy in copies:
        copy.wait()


def loop(low, high, body):
    def step(z, carry):
        body(z)
        return carry

    lax.fori_loop(low, high, step, 0)


def stencil(load, z, parts):
    values = {(p, h): load(p, z, h) for p in range(parts) for h in range(2)}
    doubled = {key: (v + v) * v for key, v in values.items()}
    linear = []
    for h in range(2):
        total = doubled[0, h]
        for p in range(1, parts):
            total = total + doubled[p, h]
        linear.append(1.0 - cross_coef * total)

    def at(p, h):
        v = values[p, h]
        other = values[p, 1 - h]
        rows = other + pltpu.roll(other, 1 if h == 0 else 7, 0)
        lanes = pltpu.roll(v, 1, 1) + pltpu.roll(v, v.shape[1] - 1, 1)
        planes = load(p, z - 1, h) + load(p, z + 1, h)
        return v, (rows + lanes) + planes + v * (doubled[p, h] + linear[h])

    return at


def grow_kernel(
    nodes, planes, hops, ext_ref, out_ref, start, cur, nxt, base, mob, inv, fac
):
    node_times, table = radau_table(nodes)
    node_times = [float(np.float32(t)) for t in node_times]
    table = np.asarray(np.asarray(table, np.float32), np.float64)
    mix = [
        [time_step * (table[m][j] - (node_times[m] if m == j else 0.0)) for j in range(nodes)]
        for m in range(nodes)
    ]
    own = hops * planes
    parts = P_SIZE
    mine = lax.axis_index("node")
    every = list(range(nodes))

    def fill(z):
        for h in range(2):
            ids = ext_ref[z, 0, h]
            for p in range(parts):
                start[p, z, h] = jnp.where(ids == float(p), 1.0, 0.0)

    loop(own - REACH, own + planes + REACH, fill)

    def pick(row_of, index):
        value = jnp.float32(row_of[0])
        for m in range(1, nodes):
            value = jnp.where(index == m, jnp.float32(row_of[m]), value)
        return value

    for step_index in range(STEPS):
        reach = REACH - step_index * STEP_REACH
        last_step = step_index + 1 == STEPS
        middle = 0.5 * time_step * STEPS

        def heat(z):
            for m in range(nodes):
                moment = (step_index + node_times[m]) * time_step
                bell = math.exp(-(((moment - middle) / middle) ** 2))
                for h in range(2):
                    theta = base_heat + (ext_ref[z, 1, h] - base_heat) * bell
                    rate = jnp.exp(activation * (1.0 - 1.0 / theta))
                    factor = (time_step * node_times[m]) * rate
                    inverse = 1.0 / (1.0 + 6.0 * factor)
                    mob[m, z, h] = rate
                    inv[m, z, h] = inverse
                    fac[m, z, h] = factor * inverse

        def span(body):
            loop(own - reach, own + planes + reach, body)

        reach -= 1
        span(heat)

        def first(z):
            at = stencil(lambda p, z, h: start[p, z, h], z, parts)
            for h in range(2):
                rates = [mob[j, z, h] for j in range(nodes)]
                mixes = []
                for m in range(nodes):
                    total = mix[m][0] * rates[0]
                    for j in range(1, nodes):
                        total = total + mix[m][j] * rates[j]
                    mixes.append(total * inv[m, z, h])
                for p in range(parts):
                    v, pull = at(p, h)
                    excess = pull - 6.0 * v
                    for m in range(nodes):
                        goal = inv[m, z, h] * v + mixes[m] * excess
                        base[m, p, z, h] = goal
                        nxt[m, p, z, h] = goal + fac[m, z, h] * pull

        span(first)
        a, b = nxt, cur
        for sweep_index in range(SWEEPS):
            last_sweep = sweep_index + 1 == SWEEPS
            if last_sweep:
                chosen = [mine if last_step else nodes - 1]
            else:
                chosen = every
            if sweep_index > 0:
                reach -= 1
                if last_sweep and last_step:
                    order = [lax.rem(mine + k, nodes) for k in range(nodes)]
                elif last_sweep:
                    order = [nodes - 1] + every[:-1]
                else:
                    order = every
                weights = [
                    [
                        mix[m][j]
                        if isinstance(m, int)
                        else pick([mix[q][(q + k) % nodes] for q in range(nodes)], m)
                        for k, j in enumerate(order)
                    ]
                    for m in order[: len(chosen)]
                ]

                def again(z, a=a, b=b, order=order, weights=weights):
                    ats = [
                        stencil(lambda p, z, h, m=m: a[m, p, z, h], z, parts) for m in order
                    ]
                    for h in range(2):
                        for p in range(parts):
                            pulls, flows = [], []
                            for at, j in zip(ats, order):
                                v, pull = at(p, h)
                                pulls.append(pull)
                                flows.append(mob[j, z, h] * (pull - 6.0 * v))
                            begin = start[p, z, h]
                            for k, row in enumerate(weights):
                                m = order[k]
                                goal = begin
                                for weight, flow in zip(row, flows):
                                    goal = goal + weight * flow
                                goal = goal * inv[m, z, h]
                                base[m, p, z, h] = goal
                                b[m, p, z, h] = goal + fac[m, z, h] * pulls[k]

                span(again)
                a, b = b, a
            for jacobi_index in range(1, JACOBI):
                reach -= 1
                final = last_sweep and jacobi_index + 1 == JACOBI

                def relax(z, a=a, b=b, chosen=chosen, final=final):
                    for m in chosen:
                        at = stencil(lambda p, z, h: a[m, p, z, h], z, parts)
                        for h in range(2):
                            for p in range(parts):
                                _, pull = at(p, h)
                                value = base[m, p, z, h] + fac[m, z, h] * pull
                                if not final:
                                    b[m, p, z, h] = value
                                elif last_step:
                                    out_ref[0, p, z - own, pl.ds(h, 8, stride=2), :] = value
                                else:
                                    start[p, z, h] = value

                span(relax)
                a, b = b, a


def on_device(grain_ids, peak_heat):
    count = lax.axis_size("space")
    nodes = lax.axis_size("node") * NODE_DEV
    planes, rows, lanes = grain_ids.shape
    assert rows == 16
    hops = -(-REACH // planes)
    extent = planes * (2 * hops + 1)
    half = (2, 8, lanes)
    pairs = 2 * hops
    vmem = pl.BlockSpec(memory_space=pltpu.VMEM)
    ext = pl.pallas_call(
        functools.partial(exchange_kernel, count, planes, hops),
        out_shape=jax.ShapeDtypeStruct((extent, 2) + half, jnp.float32),
        in_specs=[vmem, vmem],
        out_specs=vmem,
        scratch_shapes=[
            pltpu.SemaphoreType.DMA((pairs,)),
            pltpu.SemaphoreType.DMA((pairs,)),
        ],
        compiler_params=pltpu.CompilerParams(collective_id=0, has_side_effects=True),
    )(grain_ids, peak_heat)
    field = (nodes, P_SIZE, extent) + half
    coef = (nodes, extent) + half
    return pl.pallas_call(
        functools.partial(grow_kernel, nodes, planes, hops),
        out_shape=jax.ShapeDtypeStruct((NODE_DEV, P_SIZE, planes, rows, lanes), jnp.float32),
        in_specs=[vmem],
        out_specs=vmem,
        scratch_shapes=[pltpu.VMEM((P_SIZE, extent) + half, jnp.float32)]
        + [pltpu.VMEM(field, jnp.float32)] * 3
        + [pltpu.VMEM(coef, jnp.float32)] * 3,
        compiler_params=pltpu.CompilerParams(vmem_limit_bytes=60 * 2**20),
    )(ext)


def solution(mesh):
    in_specs = (P("space", None, None), P("space", None, None))
    out_specs = P("node", None, "space", None, None)
    return jax.shard_map(
        on_device, mesh=mesh, in_specs=in_specs, out_specs=out_specs, check_vma=False
    )
```

```python
import functools
import math

import jax
import jax.numpy as jnp
import numpy as np
from jax import lax
from jax.experimental import pallas as pl
from jax.experimental.pallas import tpu as pltpu
from jax.sharding import PartitionSpec as P

P_SIZE = 8
NODE_DEV = 1
SWEEPS = 3
JACOBI = 2
STEPS = 2
STEP_REACH = SWEEPS * JACOBI
REACH = STEPS * STEP_REACH

time_step = 0.25
cross_coef = 1.5
base_heat = 0.45
activation = 3.0

MESH = pl.DeviceIdType.MESH


def legendre_pair(count, point):
    before = 1.0
    current = point
    for degree in range(2, count + 1):
        following = ((2 * degree - 1) * point * current - (degree - 1) * before) / degree
        before = current
        current = following
    return (current, before)


def radau_value(count, point):
    high, low = legendre_pair(count, point)
    high_prev, low_prev = legendre_pair(count - 1, point)
    value = high - low
    slope_high = count * (point * high - low) / (point * point - 1.0)
    slope_low = (count - 1) * (point * high_prev - low_prev) / (point * point - 1.0)
    return (value, slope_high - slope_low)


def radau_table(count):
    roots = [1.0]
    for index in range(1, count):
        point = math.cos(2.0 * math.pi * index / (2 * count - 1))
        for repeat in range(100):
            value, slope = radau_value(count, point)
            point = point - value / slope
        roots.append(point)
    roots = sorted(roots)
    times_list = [(value + 1.0) / 2.0 for value in roots]
    times_list[-1] = 1.0
    table = []
    for row_index in range(count):
        upper = times_list[row_index]
        row_values = []
        for column in range(count):
            poly = [1.0]
            for other in range(count):
                if other != column:
                    scale = times_list[column] - times_list[other]
                    shifted = [0.0] + poly
                    scaled = [c * times_list[other] for c in poly] + [0.0]
                    poly = [(shifted[i] - scaled[i]) / scale for i in range(len(shifted))]
            integral_value = 0.0
            for power in range(len(poly)):
                integral_value += poly[power] * upper ** (power + 1) / (power + 1)
            row_values.append(integral_value)
        table.append(row_values)
    return (np.array(times_list), np.array(table))


def exchange_kernel(count, planes, hops, ids_ref, heat_ref, ext_ref, send, recv):
    me = lax.axis_index("space")
    offsets = [d for k in range(1, hops + 1) for d in (k, -k)]

    def target(offset):
        return {"space": lax.rem(me + offset + count, count)}

    barrier = pltpu.get_barrier_semaphore()
    for offset in offsets:
        pl.semaphore_signal(barrier, inc=1, device_id=target(offset), device_id_type=MESH)
    own = hops * planes
    for z in range(planes):
        for h in range(2):
            rows = pl.ds(h, 8, stride=2)
            ext_ref[own + z, 0, h] = ids_ref[z, rows, :].astype(jnp.float32)
            ext_ref[own + z, 1, h] = heat_ref[z, rows, :]
    pl.semaphore_wait(barrier, len(offsets))
    copies = []
    for index, offset in enumerate(offsets):
        copy = pltpu.make_async_remote_copy(
            src_ref=ext_ref.at[pl.ds(own, planes)],
            dst_ref=ext_ref.at[pl.ds(own - offset * planes, planes)],
            send_sem=send.at[index],
            recv_sem=recv.at[index],
            device_id=target(offset),
            device_id_type=MESH,
        )
        copy.start()
        copies.append(copy)
    for copy in copies:
        copy.wait()


def loop(low, high, body, unroll=1):
    rounds = (high - low) // unroll

    def step(index, carry):
        for k in range(unroll):
            body(low + index * unroll + k)
        return carry

    lax.fori_loop(0, rounds, step, 0)
    for z in range(low + rounds * unroll, high):
        body(z)


def stencil(load, z, parts):
    values = {(p, h): load(p, z, h) for p in range(parts) for h in range(2)}
    doubled = {key: (v + v) * v for key, v in values.items()}
    linear = []
    for h in range(2):
        terms = [doubled[p, h] for p in range(parts)]
        while len(terms) > 1:
            terms = [sum(terms[i + 1 : i + 2], terms[i]) for i in range(0, len(terms), 2)]
        linear.append(1.0 - cross_coef * terms[0])

    def at(p, h):
        v = values[p, h]
        other = values[p, 1 - h]
        rows = other + pltpu.roll(other, 1 if h == 0 else 7, 0)
        lanes = pltpu.roll(v, 1, 1) + pltpu.roll(v, v.shape[1] - 1, 1)
        planes = load(p, z - 1, h) + load(p, z + 1, h)
        return v, (rows + lanes) + planes + v * (doubled[p, h] + linear[h])

    return at


def grow_kernel(
    nodes, planes, hops, ext_ref, out_ref, start, cur, nxt, base, mob, inv, fac
):
    node_times, table = radau_table(nodes)
    node_times = [float(np.float32(t)) for t in node_times]
    table = np.asarray(np.asarray(table, np.float32), np.float64)
    mix = [
        [time_step * (table[m][j] - (node_times[m] if m == j else 0.0)) for j in range(nodes)]
        for m in range(nodes)
    ]
    own = hops * planes
    parts = P_SIZE
    mine = lax.axis_index("node")
    every = list(range(nodes))

    def fill(z):
        for h in range(2):
            ids = ext_ref[z, 0, h]
            for p in range(parts):
                start[p, z, h] = jnp.where(ids == float(p), 1.0, 0.0)

    loop(own - REACH, own + planes + REACH, fill)

    def pick(row_of, index):
        value = jnp.float32(row_of[0])
        for m in range(1, nodes):
            value = jnp.where(index == m, jnp.float32(row_of[m]), value)
        return value

    for step_index in range(STEPS):
        reach = REACH - step_index * STEP_REACH
        last_step = step_index + 1 == STEPS
        middle = 0.5 * time_step * STEPS

        def heat(z):
            for m in range(nodes):
                moment = (step_index + node_times[m]) * time_step
                bell = math.exp(-(((moment - middle) / middle) ** 2))
                for h in range(2):
                    theta = base_heat + (ext_ref[z, 1, h] - base_heat) * bell
                    rate = jnp.exp(activation * (1.0 - 1.0 / theta))
                    factor = (time_step * node_times[m]) * rate
                    inverse = 1.0 / (1.0 + 6.0 * factor)
                    mob[m, z, h] = rate
                    inv[m, z, h] = inverse
                    fac[m, z, h] = factor * inverse

        def span(body):
            loop(own - reach, own + planes + reach, body, 4 if nodes <= 2 else 1)

        reach -= 1
        span(heat)

        def first(z):
            at = stencil(lambda p, z, h: start[p, z, h], z, parts)
            for h in range(2):
                rates = [mob[j, z, h] for j in range(nodes)]
                mixes = []
                for m in range(nodes):
                    total = mix[m][0] * rates[0]
                    for j in range(1, nodes):
                        total = total + mix[m][j] * rates[j]
                    mixes.append(total * inv[m, z, h])
                for p in range(parts):
                    v, pull = at(p, h)
                    excess = pull - 6.0 * v
                    for m in range(nodes):
                        goal = inv[m, z, h] * v + mixes[m] * excess
                        base[m, p, z, h] = goal
                        nxt[m, p, z, h] = goal + fac[m, z, h] * pull

        span(first)
        a, b = nxt, cur
        for sweep_index in range(SWEEPS):
            last_sweep = sweep_index + 1 == SWEEPS
            if last_sweep:
                chosen = [mine if last_step else nodes - 1]
            else:
                chosen = every
            if sweep_index > 0:
                reach -= 1
                if last_sweep and last_step:
                    order = [lax.rem(mine + k, nodes) for k in range(nodes)]
                elif last_sweep:
                    order = [nodes - 1] + every[:-1]
                else:
                    order = every
                weights = [
                    [
                        mix[m][j]
                        if isinstance(m, int)
                        else pick([mix[q][(q + k) % nodes] for q in range(nodes)], m)
                        for k, j in enumerate(order)
                    ]
                    for m in order[: len(chosen)]
                ]

                def again(z, a=a, b=b, order=order, weights=weights):
                    ats = [
                        stencil(lambda p, z, h, m=m: a[m, p, z, h], z, parts) for m in order
                    ]
                    for h in range(2):
                        for p in range(parts):
                            pulls, flows = [], []
                            for at, j in zip(ats, order):
                                v, pull = at(p, h)
                                pulls.append(pull)
                                flows.append(mob[j, z, h] * (pull - 6.0 * v))
                            begin = start[p, z, h]
                            for k, row in enumerate(weights):
                                m = order[k]
                                goal = begin
                                for weight, flow in zip(row, flows):
                                    goal = goal + weight * flow
                                goal = goal * inv[m, z, h]
                                base[m, p, z, h] = goal
                                b[m, p, z, h] = goal + fac[m, z, h] * pulls[k]

                span(again)
                a, b = b, a
            for jacobi_index in range(1, JACOBI):
                reach -= 1
                final = last_sweep and jacobi_index + 1 == JACOBI

                def relax(z, a=a, b=b, chosen=chosen, final=final):
                    for m in chosen:
                        at = stencil(lambda p, z, h: a[m, p, z, h], z, parts)
                        for h in range(2):
                            for p in range(parts):
                                _, pull = at(p, h)
                                value = base[m, p, z, h] + fac[m, z, h] * pull
                                if not final:
                                    b[m, p, z, h] = value
                                elif last_step:
                                    out_ref[0, p, z - own, pl.ds(h, 8, stride=2), :] = value
                                else:
                                    start[p, z, h] = value

                span(relax)
                a, b = b, a


def on_device(grain_ids, peak_heat):
    count = lax.axis_size("space")
    nodes = lax.axis_size("node") * NODE_DEV
    planes, rows, lanes = grain_ids.shape
    assert rows == 16
    hops = -(-REACH // planes)
    extent = planes * (2 * hops + 1)
    half = (2, 8, lanes)
    pairs = 2 * hops
    vmem = pl.BlockSpec(memory_space=pltpu.VMEM)
    ext = pl.pallas_call(
        functools.partial(exchange_kernel, count, planes, hops),
        out_shape=jax.ShapeDtypeStruct((extent, 2) + half, jnp.float32),
        in_specs=[vmem, vmem],
        out_specs=vmem,
        scratch_shapes=[
            pltpu.SemaphoreType.DMA((pairs,)),
            pltpu.SemaphoreType.DMA((pairs,)),
        ],
        compiler_params=pltpu.CompilerParams(collective_id=0, has_side_effects=True),
    )(grain_ids, peak_heat)
    field = (nodes, P_SIZE, extent) + half
    coef = (nodes, extent) + half
    return pl.pallas_call(
        functools.partial(grow_kernel, nodes, planes, hops),
        out_shape=jax.ShapeDtypeStruct((NODE_DEV, P_SIZE, planes, rows, lanes), jnp.float32),
        in_specs=[vmem],
        out_specs=vmem,
        scratch_shapes=[pltpu.VMEM((P_SIZE, extent) + half, jnp.float32)]
        + [pltpu.VMEM(field, jnp.float32)] * 3
        + [pltpu.VMEM(coef, jnp.float32)] * 3,
        compiler_params=pltpu.CompilerParams(vmem_limit_bytes=60 * 2**20),
    )(ext)


def solution(mesh):
    in_specs = (P("space", None, None), P("space", None, None))
    out_specs = P("node", None, "space", None, None)
    return jax.shard_map(
        on_device, mesh=mesh, in_specs=in_specs, out_specs=out_specs, check_vma=False
    )
```

```python
import functools
import math

import jax
import jax.numpy as jnp
import numpy as np
from jax import lax
from jax.experimental import pallas as pl
from jax.experimental.pallas import tpu as pltpu
from jax.sharding import PartitionSpec as P

P_SIZE = 8
NODE_DEV = 1
SWEEPS = 3
JACOBI = 2
STEPS = 2
STEP_REACH = SWEEPS * JACOBI
REACH = STEPS * STEP_REACH

time_step = 0.25
cross_coef = 1.5
base_heat = 0.45
activation = 3.0

MESH = pl.DeviceIdType.MESH


def legendre_pair(count, point):
    before = 1.0
    current = point
    for degree in range(2, count + 1):
        following = ((2 * degree - 1) * point * current - (degree - 1) * before) / degree
        before = current
        current = following
    return (current, before)


def radau_value(count, point):
    high, low = legendre_pair(count, point)
    high_prev, low_prev = legendre_pair(count - 1, point)
    value = high - low
    slope_high = count * (point * high - low) / (point * point - 1.0)
    slope_low = (count - 1) * (point * high_prev - low_prev) / (point * point - 1.0)
    return (value, slope_high - slope_low)


def radau_table(count):
    roots = [1.0]
    for index in range(1, count):
        point = math.cos(2.0 * math.pi * index / (2 * count - 1))
        for repeat in range(100):
            value, slope = radau_value(count, point)
            point = point - value / slope
        roots.append(point)
    roots = sorted(roots)
    times_list = [(value + 1.0) / 2.0 for value in roots]
    times_list[-1] = 1.0
    table = []
    for row_index in range(count):
        upper = times_list[row_index]
        row_values = []
        for column in range(count):
            poly = [1.0]
            for other in range(count):
                if other != column:
                    scale = times_list[column] - times_list[other]
                    shifted = [0.0] + poly
                    scaled = [c * times_list[other] for c in poly] + [0.0]
                    poly = [(shifted[i] - scaled[i]) / scale for i in range(len(shifted))]
            integral_value = 0.0
            for power in range(len(poly)):
                integral_value += poly[power] * upper ** (power + 1) / (power + 1)
            row_values.append(integral_value)
        table.append(row_values)
    return (np.array(times_list), np.array(table))


def loop(low, high, body, unroll=1):
    rounds = (high - low) // unroll

    def step(index, carry):
        for k in range(unroll):
            body(low + index * unroll + k)
        return carry

    lax.fori_loop(0, rounds, step, 0)
    for z in range(low + rounds * unroll, high):
        body(z)


def stencil(load, z, parts):
    values = {(p, h): load(p, z, h) for p in range(parts) for h in range(2)}
    doubled = {key: (v + v) * v for key, v in values.items()}
    linear = []
    for h in range(2):
        terms = [doubled[p, h] for p in range(parts)]
        while len(terms) > 1:
            terms = [sum(terms[i + 1 : i + 2], terms[i]) for i in range(0, len(terms), 2)]
        linear.append(1.0 - cross_coef * terms[0])

    def at(p, h):
        v = values[p, h]
        other = values[p, 1 - h]
        rows = other + pltpu.roll(other, 1 if h == 0 else 7, 0)
        lanes = pltpu.roll(v, 1, 1) + pltpu.roll(v, v.shape[1] - 1, 1)
        planes = load(p, z - 1, h) + load(p, z + 1, h)
        return v, (rows + lanes) + planes + v * (doubled[p, h] + linear[h])

    return at


def grow_kernel(
    count, nodes, planes, hops, skew, ids_ref, heat_ref, out_ref,
    ext_ref, starts, stages, bases, mob, inv, fac, send, recv,
):
    node_times, table = radau_table(nodes)
    node_times = [float(np.float32(t)) for t in node_times]
    table = np.asarray(np.asarray(table, np.float32), np.float64)
    mix = [
        [time_step * (table[m][j] - (node_times[m] if m == j else 0.0)) for j in range(nodes)]
        for m in range(nodes)
    ]
    own = hops * planes
    parts = P_SIZE
    me = lax.axis_index("space")
    mine = lax.axis_index("node")
    every = list(range(nodes))
    unroll = 4 if skew else 1

    offsets = [d for k in range(1, hops + 1) for d in (k, -k)]

    def target(offset):
        return {"space": lax.rem(me + offset + count, count)}

    barrier = pltpu.get_barrier_semaphore()
    for offset in offsets:
        pl.semaphore_signal(barrier, inc=1, device_id=target(offset), device_id_type=MESH)
    for z in range(planes):
        for h in range(2):
            rows = pl.ds(h, 8, stride=2)
            ext_ref[own + z, 0, h] = ids_ref[z, rows, :].astype(jnp.float32)
            ext_ref[own + z, 1, h] = heat_ref[z, rows, :]
    pl.semaphore_wait(barrier, len(offsets))
    copies = []
    for index, offset in enumerate(offsets):
        copy = pltpu.make_async_remote_copy(
            src_ref=ext_ref.at[pl.ds(own, planes)],
            dst_ref=ext_ref.at[pl.ds(own - offset * planes, planes)],
            send_sem=send.at[index],
            recv_sem=recv.at[index],
            device_id=target(offset),
            device_id_type=MESH,
        )
        copy.start()
        copies.append(copy)

    def fill(z):
        for h in range(2):
            ids = ext_ref[z, 0, h]
            for p in range(parts):
                starts[0, p, z, h] = jnp.where(ids == float(p), 1.0, 0.0)

    def pick(row_of, index):
        value = jnp.float32(row_of[0])
        for m in range(1, nodes):
            value = jnp.where(index == m, jnp.float32(row_of[m]), value)
        return value

    def heat(step_index, z):
        middle = 0.5 * time_step * STEPS
        for m in range(nodes):
            moment = (step_index + node_times[m]) * time_step
            bell = math.exp(-(((moment - middle) / middle) ** 2))
            for h in range(2):
                theta = base_heat + (ext_ref[z, 1, h] - base_heat) * bell
                rate = jnp.exp(activation * (1.0 - 1.0 / theta))
                factor = (time_step * node_times[m]) * rate
                inverse = 1.0 / (1.0 + 6.0 * factor)
                mob[m, z, h] = rate
                inv[m, z, h] = inverse
                fac[m, z, h] = factor * inverse

    def prepare(z):
        fill(z)
        heat(0, z)

    def level(step_index, number):
        last_step = step_index + 1 == STEPS
        sweep_index, jacobi_index = divmod(number, JACOBI)
        last_sweep = sweep_index + 1 == SWEEPS
        start = starts.at[step_index % starts.shape[0]]
        following = starts.at[(step_index + 1) % starts.shape[0]]
        base = bases.at[sweep_index % bases.shape[0]]
        a = stages.at[(number - 1) % stages.shape[0]]
        b = stages.at[number % stages.shape[0]]

        def first(z):
            at = stencil(lambda p, z, h: start[p, z, h], z, parts)
            for h in range(2):
                rates = [mob[j, z, h] for j in range(nodes)]
                mixes = []
                for m in range(nodes):
                    total = mix[m][0] * rates[0]
                    for j in range(1, nodes):
                        total = total + mix[m][j] * rates[j]
                    mixes.append(total * inv[m, z, h])
                for p in range(parts):
                    v, pull = at(p, h)
                    excess = pull - 6.0 * v
                    for m in range(nodes):
                        goal = inv[m, z, h] * v + mixes[m] * excess
                        base[m, p, z, h] = goal
                        b[m, p, z, h] = goal + fac[m, z, h] * pull

        if not last_sweep:
            order, chosen = every, every
        elif last_step:
            order = [lax.rem(mine + k, nodes) for k in range(nodes)]
            chosen = order[:1]
        else:
            order = [nodes - 1] + every[:-1]
            chosen = order[:1]
        weights = [
            [
                mix[m][j]
                if isinstance(m, int)
                else pick([mix[q][(q + k) % nodes] for q in range(nodes)], m)
                for k, j in enumerate(order)
            ]
            for m in chosen
        ]

        def again(z):
            ats = [stencil(lambda p, z, h, m=m: a[m, p, z, h], z, parts) for m in order]
            for h in range(2):
                for p in range(parts):
                    pulls, flows = [], []
                    for at, j in zip(ats, order):
                        v, pull = at(p, h)
                        pulls.append(pull)
                        flows.append(mob[j, z, h] * (pull - 6.0 * v))
                    begin = start[p, z, h]
                    for k, row in enumerate(weights):
                        m = order[k]
                        goal = begin
                        for weight, flow in zip(row, flows):
                            goal = goal + weight * flow
                        goal = goal * inv[m, z, h]
                        base[m, p, z, h] = goal
                        b[m, p, z, h] = goal + fac[m, z, h] * pulls[k]

        final = number + 1 == STEP_REACH

        def relax(z):
            for m in chosen:
                at = stencil(lambda p, z, h: a[m, p, z, h], z, parts)
                for h in range(2):
                    for p in range(parts):
                        _, pull = at(p, h)
                        value = base[m, p, z, h] + fac[m, z, h] * pull
                        if not final:
                            b[m, p, z, h] = value
                        elif last_step:
                            out_ref[0, p, z - own, pl.ds(h, 8, stride=2), :] = value
                        else:
                            following[p, z, h] = value

        if jacobi_index > 0:
            return relax
        return again if sweep_index > 0 else first

    done = 0
    if skew:
        loop(own, own + planes, prepare, 2)
        copies[0].wait_recv()
        copies[1].wait_recv()
        loop(own - planes, own, prepare, 2)
        loop(own + planes, own + 2 * planes, prepare, 2)
        for number in range(STEP_REACH):
            reach = planes - 1 - number
            if planes + 2 * reach > 0:
                loop(own - reach, own + planes + reach, level(0, number), 2)

        def ring(turn, carry):
            distance = (2 + turn // 2) * planes
            side = lax.rem(turn, 2)
            pltpu.make_async_remote_copy(
                src_ref=ext_ref.at[pl.ds(own, planes)],
                dst_ref=ext_ref.at[pl.ds(own, planes)],
                send_sem=send.at[2 + turn],
                recv_sem=recv.at[2 + turn],
                device_id=target(1),
                device_id_type=MESH,
            ).wait_recv()
            low = own + jnp.where(side == 0, -distance, distance)
            inward = jnp.where(side == 0, 1, -1)
            for k in range(planes):
                prepare(low + k)
            for number in range(STEP_REACH):
                body = level(0, number)
                for k in range(planes):
                    body(low + inward * (number + 1) + k)
            return carry

        lax.fori_loop(0, 2 * (hops - 1), ring, 0)
        done = 1
    else:
        for copy in copies:
            copy.wait_recv()
        loop(own - REACH, own + planes + REACH, fill)
    for step_index in range(done, STEPS):
        reach = REACH - step_index * STEP_REACH - 1
        loop(own - reach, own + planes + reach, functools.partial(heat, step_index), unroll)
        for number in range(STEP_REACH):
            body = level(step_index, number)
            loop(own - reach + number, own + planes + reach - number, body, unroll)
    for copy in copies:
        copy.wait_send()


def on_device(grain_ids, peak_heat):
    count = lax.axis_size("space")
    nodes = lax.axis_size("node") * NODE_DEV
    planes, rows, lanes = grain_ids.shape
    assert rows == 16
    hops = -(-REACH // planes)
    extent = planes * (2 * hops + 1)
    skew = nodes <= 2 and hops * planes == REACH and planes + 2 * (planes - STEP_REACH) >= 0
    half = (2, 8, lanes)
    pairs = 2 * hops
    vmem = pl.BlockSpec(memory_space=pltpu.VMEM)
    field = (nodes, P_SIZE, extent) + half
    coef = (nodes, extent) + half
    return pl.pallas_call(
        functools.partial(grow_kernel, count, nodes, planes, hops, skew),
        out_shape=jax.ShapeDtypeStruct((NODE_DEV, P_SIZE, planes, rows, lanes), jnp.float32),
        in_specs=[vmem, vmem],
        out_specs=vmem,
        scratch_shapes=[
            pltpu.VMEM((extent, 2) + half, jnp.float32),
            pltpu.VMEM((2 if skew else 1, P_SIZE, extent) + half, jnp.float32),
            pltpu.VMEM(((STEP_REACH - 1 if skew else 2),) + field, jnp.float32),
            pltpu.VMEM(((SWEEPS if skew else 1),) + field, jnp.float32),
        ]
        + [pltpu.VMEM(coef, jnp.float32)] * 3
        + [pltpu.SemaphoreType.DMA((pairs,))] * 2,
        compiler_params=pltpu.CompilerParams(
            collective_id=0, has_side_effects=True, vmem_limit_bytes=60 * 2**20
        ),
    )(grain_ids, peak_heat)


def solution(mesh):
    in_specs = (P("space", None, None), P("space", None, None))
    out_specs = P("node", None, "space", None, None)
    return jax.shard_map(
        on_device, mesh=mesh, in_specs=in_specs, out_specs=out_specs, check_vma=False
    )
```
